32 devices in a mesh: gx: 4 (over y, x), gy: 8 (over z, core).
Axes of the slice: x: 2, y: 2, z: 4, core: 2. Of those that a mesh axis runs over, the one named last changes fastest.
Arguments:
- volume: bfloat16 [32, 8, 256, 256], P(None, 'gx', 'gy'), may hold values from -6 to 6
- conv1_weight: bfloat16 [3, 3, 3, 32, 64], replicated, may hold values from -0.21875 to 0.21875
- conv1_bias: float32 [64], replicated, may hold values from -3 to 3
- conv2_weight: bfloat16 [3, 3, 3, 64, 128], replicated, may hold values from -0.15625 to 0.15625
- conv2_bias: float32 [128], replicated, may hold values from -3 to 3
Outputs:
- activation: bfloat16 [4, 128, 128, 128], P('gx', 'gy')
The draws below stay inside these ranges and needn't reach their ends.
All inputs are finite; a program needn't handle non-finite values.
Results may differ from the reference program's by a relative error of at most 0.0045.
Values may be sent and summed in bfloat16 or wider, within the bound.
A program may use at most 256 MiB of HBM per device.

```python
import jax
import jax.numpy as jnp
from jax import lax

CIN = 32
CMID = 64
COUT = 128
NY = 256
NZ = 256
NX = 8


def block_scale(own_key, shape, pieces, low, largest):
    def one(position, shards_of):
        steps = jax.random.uniform(jax.random.fold_in(jax.random.fold_in(own_key, 6), position), (shards_of,), jnp.float32, low / len(pieces), largest / len(pieces))
        return jnp.repeat(jnp.exp(steps), shape[position] // shards_of).reshape((-1,) + (1,) * (len(shape) - position - 1))

    factor_of = one(*pieces[0])
    for cut in pieces[1:]:
        factor_of = factor_of * one(*cut)
    return factor_of


def noise(key, shape, deviation, limit, shards=(), dtype=jnp.bfloat16):
    gain = block_scale(key, shape, shards, -0.22, 0.18) if shards else 1.0
    array = jax.random.normal(key, shape, jnp.float32) * deviation * gain
    return jnp.minimum(jnp.maximum(array, -limit), limit).astype(dtype)


def setup_inputs(seed: int = 0) -> dict:
    seeds = jax.random.split(jax.random.key(seed), 6)
    return {
        "volume": noise(seeds[0], (CIN, NX, NY, NZ), 1.0, 6.0, ((1, 4), (2, 8))),
        "conv1_weight": noise(seeds[1], (3, 3, 3, CIN, CMID), (27 * CIN) ** -0.5, 0.21875),
        "conv1_bias": noise(seeds[2], (CMID,), 0.5, 3.0, (), jnp.float32),
        "conv2_weight": noise(seeds[3], (3, 3, 3, CMID, COUT), (27 * CMID) ** -0.5, 0.15625),
        "conv2_bias": noise(seeds[4], (COUT,), 0.5, 3.0, (), jnp.float32),
    }


leak_slope = 0.3


def leaky(values):
    return jnp.where(values > 0, values, leak_slope * values)


def reference(volume, conv1_weight, conv1_bias, conv2_weight, conv2_bias):
    source = volume.astype(jnp.float32)[None]
    first = lax.conv_general_dilated(source, conv1_weight.astype(jnp.float32), (2, 2, 2), ((1, 0), (1, 0), (1, 0)), dimension_numbers=("NCDHW", "DHWIO", "NCDHW"), precision=lax.Precision.HIGHEST)[0]
    feature = leaky(first + conv1_bias.astype(jnp.float32)[:, None, None, None]).astype(jnp.bfloat16)
    total = lax.conv_general_dilated(feature.astype(jnp.float32)[None], conv2_weight.astype(jnp.float32), (1, 1, 1), ((1, 1), (1, 1), (1, 1)), dimension_numbers=("NCDHW", "DHWIO", "DNCHW"), precision=lax.Precision.HIGHEST)[:, 0]
    return leaky(total + conv2_bias.astype(jnp.float32)[None, :, None, None]).astype(jnp.bfloat16)
```

```python
import functools

import jax
import jax.numpy as jnp
from jax import lax
from jax.experimental import pallas as pl
from jax.experimental.pallas import tpu as pltpu
from jax.sharding import PartitionSpec as P

leak_slope = 0.3
MESH = pl.DeviceIdType.MESH
LANES = 128


def leaky(values):
    return jnp.where(values > 0, values, leak_slope * values)


def shift_right(values):
    lane = lax.broadcasted_iota(jnp.int32, values.shape, 1)
    return jnp.where(lane == 0, 0.0, pltpu.roll(values, 1, 1))


def shift_left(values):
    lane = lax.broadcasted_iota(jnp.int32, values.shape, 1)
    return jnp.where(lane == LANES - 1, 0.0, pltpu.roll(values, LANES - 1, 1))


def kernel(groups_x, groups_y, chunks, vol, w1, b1, w2, b2, out,
           cells, part_out, part_in, own, feats, result,
           cell_sems, part_sems, feat_sems, edge_sems, send_sems, recv_sems):
    gx = lax.axis_index("gx")
    gy = lax.axis_index("gy")
    has_left = gx > 0
    has_right = gx < groups_x - 1
    has_up = gy > 0
    has_down = gy < groups_y - 1
    rows = own.shape[0]
    step = rows // chunks
    in_rows = vol.shape[2]
    cin = vol.shape[0]
    cmid = own.shape[1]
    fw = result.shape[2]

    feats[...] = jnp.zeros_like(feats)
    part_in[...] = jnp.zeros_like(part_in)
    cells[0] = jnp.zeros(cells.shape[1:], cells.dtype)

    barrier = pltpu.get_barrier_semaphore()

    def greet(x, y):
        pl.semaphore_signal(barrier, inc=1, device_id=(x, y), device_id_type=MESH)

    for d in range(1, groups_y):
        greet(gx, lax.rem(gy + d, groups_y))
    for dx, okx in ((-1, has_left), (1, has_right)):
        for dy, oky in ((-1, has_up), (0, None), (1, has_down)):
            @pl.when(okx if oky is None else jnp.logical_and(okx, oky))
            def _():
                greet(gx + dx, gy + dy)

    sides_y = 1 + has_up.astype(jnp.int32) + has_down.astype(jnp.int32)
    sides_x = has_left.astype(jnp.int32) + has_right.astype(jnp.int32)

    row = lax.broadcasted_iota(jnp.int32, (2 * LANES, 2 * LANES), 0)
    col = lax.broadcasted_iota(jnp.int32, (2 * LANES, 2 * LANES), 1)
    picked = jnp.where(col < LANES, 2 * col, 2 * col - (2 * LANES - 1))
    select = (row == picked).astype(jnp.float32).astype(jnp.bfloat16)

    def split(block):
        for p in range(2):
            part = vol[:, p, pl.ds(block * 16, 16), :].astype(jnp.float32)
            turned = jnp.swapaxes(part, 0, 1).astype(jnp.bfloat16)
            flat = turned.reshape(16 * cin, 2 * LANES)
            both = jnp.dot(flat, select, preferred_element_type=jnp.float32)
            both = both.astype(jnp.bfloat16)
            for q in range(2):
                cells[pl.ds(1 + block * 16, 16), p, q] = (
                    both[:, q * LANES:(q + 1) * LANES].reshape(16, cin, LANES))

    blocks = in_rows // 16
    split(blocks - 1)
    pl.semaphore_wait(barrier, groups_y - 1 + sides_x * sides_y)

    def cell_copy(y):
        return pltpu.make_async_remote_copy(
            src_ref=cells.at[in_rows], dst_ref=cells.at[0],
            send_sem=cell_sems.at[0], recv_sem=cell_sems.at[1],
            device_id=(gx, y), device_id_type=MESH)

    @pl.when(has_down)
    def _():
        cell_copy(gy + 1).start()

    for block in range(blocks - 1):
        split(block)

    def part_copy(c, x):
        span = pl.ds(c * step, step)
        return pltpu.make_async_remote_copy(
            src_ref=part_out.at[span], dst_ref=part_in.at[span],
            send_sem=part_sems.at[0, c], recv_sem=part_sems.at[1, c],
            device_id=(x, gy), device_id_type=MESH)

    def first_row(j, carry):
        window = cells[pl.ds(2 * j, 3)].reshape(12 * cin, LANES)
        y = jnp.dot(w1[...], window, preferred_element_type=jnp.float32)
        own[j] = y[:cmid] + shift_right(y[cmid:2 * cmid])
        part_out[j] = (y[2 * cmid:3 * cmid] + shift_right(y[3 * cmid:])).astype(jnp.bfloat16)
        return carry

    for c in reversed(range(chunks)):
        if c == 0:
            @pl.when(has_up)
            def _():
                cell_copy(gy).wait_recv()
        lax.fori_loop(c * step, (c + 1) * step, first_row, 0)

        @pl.when(has_right)
        def _():
            part_copy(c, gx + 1).start()

    def feat_copy(c, side, x):
        span = pl.ds(1 + c * step, step)
        return pltpu.make_async_remote_copy(
            src_ref=feats.at[span, 1], dst_ref=feats.at[span, 2 - 2 * side],
            send_sem=feat_sems.at[0, side, c], recv_sem=feat_sems.at[1, side, c],
            device_id=(x, gy), device_id_type=MESH)

    def edge_copy(down, dx, x, y):
        return pltpu.make_async_remote_copy(
            src_ref=feats.at[rows if down else 1, 1],
            dst_ref=feats.at[0 if down else rows + 1, 1 - dx],
            send_sem=edge_sems.at[0, down, dx + 1], recv_sem=edge_sems.at[1, down, dx + 1],
            device_id=(x, y), device_id_type=MESH)

    def both_of(a, b):
        return b if a is None else jnp.logical_and(a, b)

    def send_edges(down):
        for dx, okx in ((0, None), (-1, has_left), (1, has_right)):
            @pl.when(both_of(okx, has_down if down else has_up))
            def _():
                edge_copy(down, dx, gx + dx, gy + (1 if down else -1)).start()

    def finish_row(j, carry):
        value = own[j] + part_in[j].astype(jnp.float32) + b1[...]
        feats[j + 1, 1] = leaky(value).astype(jnp.bfloat16)
        return carry

    for c in reversed(range(chunks)):
        @pl.when(has_left)
        def _():
            part_copy(c, gx).wait_recv()
        lax.fori_loop(c * step, (c + 1) * step, finish_row, 0)
        if c == chunks - 1:
            send_edges(1)
        if c == 0:
            send_edges(0)

        @pl.when(has_left)
        def _():
            feat_copy(c, 0, gx - 1).start()

        @pl.when(has_right)
        def _():
            feat_copy(c, 1, gx + 1).start()

    def result_copy(c, peer, src_group, y, sem_peer):
        span = pl.ds(c * step, step)
        return pltpu.make_async_remote_copy(
            src_ref=result.at[span, peer], dst_ref=out.at[src_group, span],
            send_sem=send_sems.at[c, peer], recv_sem=recv_sems.at[c, sem_peer],
            device_id=(gx, y), device_id_type=MESH)

    def second_row(j, carry):
        window = feats[pl.ds(j, 3)].reshape(9 * cmid, LANES)
        y = jnp.dot(w2[...], window, preferred_element_type=jnp.float32)
        n = y.shape[0] // 3
        total = shift_right(y[:n]) + y[n:2 * n] + shift_left(y[2 * n:]) + b2[...]
        result[j] = leaky(total).reshape(groups_y, fw, LANES).astype(jnp.bfloat16)
        return carry

    def wait_feats(c):
        @pl.when(has_right)
        def _():
            feat_copy(c, 0, gx).wait_recv()

        @pl.when(has_left)
        def _():
            feat_copy(c, 1, gx).wait_recv()

    def wait_edges(down):
        for dx, okx in ((0, None), (-1, has_right), (1, has_left)):
            @pl.when(both_of(okx, has_up if down else has_down))
            def _():
                edge_copy(down, dx, gx, gy).wait_recv()

    wait_feats(chunks - 1)
    wait_edges(0)
    for c in reversed(range(chunks)):
        if c > 0:
            wait_feats(c - 1)
        else:
            wait_edges(1)
        lax.fori_loop(c * step, (c + 1) * step, second_row, 0)

        def send(d, carry):
            peer = lax.rem(gy + d, groups_y)
            result_copy(c, peer, gy, peer, gy).start()
            return carry

        lax.fori_loop(1, groups_y, send, 0)

    out[gy] = result[:, gy]

    @pl.when(has_down)
    def _():
        cell_copy(gy).wait_send()

    for c in range(chunks):
        @pl.when(has_right)
        def _():
            part_copy(c, gx).wait_send()
            feat_copy(c, 1, gx).wait_send()

        @pl.when(has_left)
        def _():
            feat_copy(c, 0, gx).wait_send()

    for down in range(2):
        for dx, okx in ((0, None), (-1, has_left), (1, has_right)):
            @pl.when(both_of(okx, has_down if down else has_up))
            def _():
                edge_copy(down, dx, gx, gy).wait_send()

    for c in reversed(range(chunks)):
        def finish(d, carry):
            peer = lax.rem(gy + d, groups_y)
            copy = result_copy(c, peer, peer, gy, peer)
            copy.wait_send()
            copy.wait_recv()
            return carry

        lax.fori_loop(1, groups_y, finish, 0)


def on_device(volume, conv1_weight, conv1_bias, conv2_weight, conv2_bias):
    groups_x = lax.axis_size("gx")
    groups_y = lax.axis_size("gy")
    cin, planes, in_rows, nz = volume.shape
    cmid = conv1_weight.shape[4]
    cout = conv2_weight.shape[4]
    rows = in_rows // 2
    fw = cout // groups_y
    chunks = 4

    w = conv1_weight.transpose(1, 0, 2, 3, 4)
    own_main = w[:, 1:3, 1:3]
    own_shift = jnp.pad(w[:, 1:3, 0:1], ((0, 0), (0, 0), (1, 0), (0, 0), (0, 0)))
    part_main = jnp.pad(w[:, 0:1, 1:3], ((0, 0), (1, 0), (0, 0), (0, 0), (0, 0)))
    part_shift = jnp.pad(w[:, 0:1, 0:1], ((0, 0), (1, 0), (1, 0), (0, 0), (0, 0)))
    w1 = jnp.concatenate([own_main, own_shift, part_main, part_shift], axis=4)
    w1 = w1.reshape(12 * cin, 4 * cmid).T
    w2 = conv2_weight.transpose(2, 4, 1, 0, 3).reshape(3 * cout, 9 * cmid)

    vmem = pl.BlockSpec(memory_space=pltpu.VMEM)
    moved = pl.pallas_call(
        functools.partial(kernel, groups_x, groups_y, chunks),
        out_shape=jax.ShapeDtypeStruct((groups_y, rows, fw, LANES), jnp.bfloat16),
        in_specs=[vmem] * 5,
        out_specs=vmem,
        scratch_shapes=[
            pltpu.VMEM((in_rows + 1, 2, 2, cin, LANES), jnp.bfloat16),
            pltpu.VMEM((rows, cmid, LANES), jnp.bfloat16),
            pltpu.VMEM((rows, cmid, LANES), jnp.bfloat16),
            pltpu.VMEM((rows, cmid, LANES), jnp.float32),
            pltpu.VMEM((rows + 2, 3, cmid, LANES), jnp.bfloat16),
            pltpu.VMEM((rows, groups_y, fw, LANES), jnp.bfloat16),
            pltpu.SemaphoreType.DMA((2,)),
            pltpu.SemaphoreType.DMA((2, chunks)),
            pltpu.SemaphoreType.DMA((2, 2, chunks)),
            pltpu.SemaphoreType.DMA((2, 2, 3)),
            pltpu.SemaphoreType.DMA((chunks, groups_y)),
            pltpu.SemaphoreType.DMA((chunks, groups_y)),
        ],
        compiler_params=pltpu.CompilerParams(
            collective_id=0, has_side_effects=True, vmem_limit_bytes=40 * 1024 * 1024),
    )(volume, w1, conv1_bias.reshape(cmid, 1), w2, conv2_bias.reshape(cout, 1))
    return moved.transpose(2, 0, 1, 3).reshape(1, fw, groups_y * rows, LANES)


def solution(mesh):
    return jax.shard_map(
        on_device,
        mesh=mesh,
        in_specs=(P(None, "gx", "gy", None), P(), P(), P(), P()),
        out_specs=P("gx", "gy", None, None),
        check_vma=False,
    )
```

```python
import functools

import jax
import jax.numpy as jnp
from jax import lax
from jax.experimental import pallas as pl
from jax.experimental.pallas import tpu as pltpu
from jax.sharding import PartitionSpec as P

leak_slope = 0.3
MESH = pl.DeviceIdType.MESH
LANES = 128


def leaky(values):
    return jnp.where(values > 0, values, leak_slope * values)


def shift_right(values):
    lane = lax.broadcasted_iota(jnp.int32, values.shape, 1)
    return jnp.where(lane == 0, 0.0, pltpu.roll(values, 1, 1))


def shift_left(values):
    lane = lax.broadcasted_iota(jnp.int32, values.shape, 1)
    return jnp.where(lane == LANES - 1, 0.0, pltpu.roll(values, LANES - 1, 1))


def kernel(groups_x, groups_y, chunks, vol, first_weight, b1, second_weight, b2, out,
           cells, part_out, part_in, own, own_out, own_in, feats, result, w1, w2,
           cell_sems, part_sems, feat_sems, edge_sems, send_sems, recv_sems):
    gx = lax.axis_index("gx")
    gy = lax.axis_index("gy")
    has_left = gx > 0
    has_right = gx < groups_x - 1
    has_up = gy > 0
    has_down = gy < groups_y - 1
    rows = own.shape[0]
    step = rows // chunks
    in_rows = vol.shape[2]
    cin = vol.shape[0]
    cmid = own.shape[1]
    fw = result.shape[2]

    feats[...] = jnp.zeros_like(feats)
    part_in[...] = jnp.zeros_like(part_in)
    cells[0] = jnp.zeros(cells.shape[1:], cells.dtype)

    barrier = pltpu.get_barrier_semaphore()

    def greet(x, y):
        pl.semaphore_signal(barrier, inc=1, device_id=(x, y), device_id_type=MESH)

    for d in range(1, groups_y):
        greet(gx, lax.rem(gy + d, groups_y))
    for dx, okx in ((-1, has_left), (1, has_right)):
        for dy, oky in ((-1, has_up), (0, None), (1, has_down)):
            @pl.when(okx if oky is None else jnp.logical_and(okx, oky))
            def _():
                greet(gx + dx, gy + dy)

    sides_y = 1 + has_up.astype(jnp.int32) + has_down.astype(jnp.int32)
    sides_x = has_left.astype(jnp.int32) + has_right.astype(jnp.int32)

    def turned(pieces):
        return jnp.concatenate(pieces, axis=0).astype(jnp.float32).T.astype(jnp.bfloat16)

    blank = jnp.zeros((cin, cmid), jnp.bfloat16)
    taps = [(b, p, q) for b in range(3) for p in range(2) for q in range(2)]
    kinds = (
        [first_weight[p + 1, b, q + 1] for b, p, q in taps],
        [first_weight[p + 1, b, 0] if q == 1 else blank for b, p, q in taps],
        [first_weight[0, b, q + 1] if p == 1 else blank for b, p, q in taps],
        [first_weight[0, b, 0] if p == 1 and q == 1 else blank for b, p, q in taps],
    )
    for place, pieces in enumerate(kinds):
        w1[place * cmid:(place + 1) * cmid, :] = turned(pieces)

    row = lax.broadcasted_iota(jnp.int32, (2 * LANES, 2 * LANES), 0)
    col = lax.broadcasted_iota(jnp.int32, (2 * LANES, 2 * LANES), 1)
    picked = jnp.where(col < LANES, 2 * col, 2 * col - (2 * LANES - 1))
    select = (row == picked).astype(jnp.float32).astype(jnp.bfloat16)

    def split(block):
        for p in range(2):
            part = vol[:, p, pl.ds(block * 16, 16), :].astype(jnp.float32)
            turned = jnp.swapaxes(part, 0, 1).astype(jnp.bfloat16)
            flat = turned.reshape(16 * cin, 2 * LANES)
            both = jnp.dot(flat, select, preferred_element_type=jnp.float32)
            both = both.astype(jnp.bfloat16)
            for q in range(2):
                cells[pl.ds(1 + block * 16, 16), p, q] = (
                    both[:, q * LANES:(q + 1) * LANES].reshape(16, cin, LANES))

    blocks = in_rows // 16
    split(blocks - 1)
    pl.semaphore_wait(barrier, groups_y - 1 + sides_x * sides_y)

    def cell_copy(y):
        return pltpu.make_async_remote_copy(
            src_ref=cells.at[in_rows], dst_ref=cells.at[0],
            send_sem=cell_sems.at[0], recv_sem=cell_sems.at[1],
            device_id=(gx, y), device_id_type=MESH)

    @pl.when(has_down)
    def _():
        cell_copy(gy + 1).start()

    def part_copy(c, x):
        span = pl.ds(c * step, step)
        return pltpu.make_async_remote_copy(
            src_ref=part_out.at[span], dst_ref=part_in.at[span],
            send_sem=part_sems.at[0, c], recv_sem=part_sems.at[1, c],
            device_id=(x, gy), device_id_type=MESH)

    def own_copy(c, x):
        span = pl.ds(c * step, step)
        return pltpu.make_async_remote_copy(
            src_ref=own_out.at[span], dst_ref=own_in.at[span],
            send_sem=feat_sems.at[0, 0, c], recv_sem=feat_sems.at[1, 0, c],
            device_id=(x, gy), device_id_type=MESH)

    def first_rows(j):
        window = jnp.concatenate(
            [cells[2 * (j + h):2 * (j + h) + 3].reshape(12 * cin, LANES) for h in range(2)], axis=1)
        y = jnp.dot(w1[...], window, preferred_element_type=jnp.float32)
        for h in range(2):
            z = y[:, h * LANES:(h + 1) * LANES]
            mine = z[:cmid] + shift_right(z[cmid:2 * cmid])
            own[j + h] = mine
            own_out[j + h] = mine.astype(jnp.bfloat16)
            part_out[j + h] = (
                z[2 * cmid:3 * cmid] + shift_right(z[3 * cmid:])).astype(jnp.bfloat16)

    ready = blocks - 1
    for c in reversed(range(chunks)):
        while ready > 0 and 2 * c * step - 1 < ready * 16:
            ready -= 1
            split(ready)
        if c == 0:
            @pl.when(has_up)
            def _():
                cell_copy(gy).wait_recv()
        for j in range(c * step, (c + 1) * step, 2):
            first_rows(j)

        @pl.when(has_right)
        def _():
            part_copy(c, gx + 1).start()

        @pl.when(has_left)
        def _():
            own_copy(c, gx - 1).start()

    filters = w2.shape[0] // 3
    for e in range(3):
        w2[e * filters:(e + 1) * filters, :] = turned(
            [second_weight[a, b, e] for b in range(3) for a in range(3)])

    def feat_copy(c, x):
        span = pl.ds(1 + c * step, step)
        return pltpu.make_async_remote_copy(
            src_ref=feats.at[span, 1], dst_ref=feats.at[span, 0],
            send_sem=feat_sems.at[0, 1, c], recv_sem=feat_sems.at[1, 1, c],
            device_id=(x, gy), device_id_type=MESH)

    def edge_copy(down, dx, x, y):
        return pltpu.make_async_remote_copy(
            src_ref=feats.at[rows if down else 1, 1],
            dst_ref=feats.at[0 if down else rows + 1, 1 - dx],
            send_sem=edge_sems.at[0, down, dx + 1], recv_sem=edge_sems.at[1, down, dx + 1],
            device_id=(x, y), device_id_type=MESH)

    def both_of(a, b):
        return b if a is None else jnp.logical_and(a, b)

    def send_edges(down):
        for dx, okx in ((0, None), (-1, has_left), (1, has_right)):
            @pl.when(both_of(okx, has_down if down else has_up))
            def _():
                edge_copy(down, dx, gx + dx, gy + (1 if down else -1)).start()

    def finish_row(j, carry):
        value = own[j] + part_in[j].astype(jnp.float32) + b1[...]
        feats[j + 1, 1] = leaky(value).astype(jnp.bfloat16)
        return carry

    for c in reversed(range(chunks)):
        @pl.when(has_left)
        def _():
            part_copy(c, gx).wait_recv()
        lax.fori_loop(c * step, (c + 1) * step, finish_row, 0)
        if c == chunks - 1:
            send_edges(1)
        if c == 0:
            send_edges(0)

        @pl.when(has_right)
        def _():
            feat_copy(c, gx + 1).start()

    def next_row(j, carry):
        value = own_in[j].astype(jnp.float32) + part_out[j].astype(jnp.float32) + b1[...]
        feats[j + 1, 2] = leaky(value).astype(jnp.bfloat16)
        return carry

    def result_copy(c, peer, src_group, y, sem_peer):
        span = pl.ds(c * step, step)
        return pltpu.make_async_remote_copy(
            src_ref=result.at[span, peer], dst_ref=out.at[src_group, span],
            send_sem=send_sems.at[c, peer], recv_sem=recv_sems.at[c, sem_peer],
            device_id=(gx, y), device_id_type=MESH)

    def second_rows(j):
        window = jnp.concatenate(
            [feats[j + h:j + h + 3].reshape(9 * cmid, LANES) for h in range(2)], axis=1)
        y = jnp.dot(w2[...], window, preferred_element_type=jnp.float32)
        for h in range(2):
            z = y[:, h * LANES:(h + 1) * LANES]
            total = (shift_right(z[:filters]) + z[filters:2 * filters]
                     + shift_left(z[2 * filters:]) + b2[...])
            result[j + h] = leaky(total).reshape(groups_y, fw, LANES).astype(jnp.bfloat16)

    def wait_feats(c):
        @pl.when(has_right)
        def _():
            own_copy(c, gx).wait_recv()
            lax.fori_loop(c * step, (c + 1) * step, next_row, 0)

        @pl.when(has_left)
        def _():
            feat_copy(c, gx).wait_recv()

    def wait_edges(down):
        for dx, okx in ((0, None), (-1, has_right), (1, has_left)):
            @pl.when(both_of(okx, has_up if down else has_down))
            def _():
                edge_copy(down, dx, gx, gy).wait_recv()

    wait_feats(chunks - 1)
    wait_edges(0)
    for c in reversed(range(chunks)):
        if c > 0:
            wait_feats(c - 1)
        else:
            wait_edges(1)
        for j in range(c * step, (c + 1) * step, 2):
            second_rows(j)

        def send(d, carry):
            peer = lax.rem(gy + d, groups_y)
            result_copy(c, peer, gy, peer, gy).start()
            return carry

        lax.fori_loop(1, groups_y, send, 0)

    out[gy] = result[:, gy]

    @pl.when(has_down)
    def _():
        cell_copy(gy).wait_send()

    for c in range(chunks):
        @pl.when(has_right)
        def _():
            part_copy(c, gx).wait_send()
            feat_copy(c, gx).wait_send()

        @pl.when(has_left)
        def _():
            own_copy(c, gx).wait_send()

    for down in range(2):
        for dx, okx in ((0, None), (-1, has_left), (1, has_right)):
            @pl.when(both_of(okx, has_down if down else has_up))
            def _():
                edge_copy(down, dx, gx, gy).wait_send()

    for c in reversed(range(chunks)):
        def finish(d, carry):
            peer = lax.rem(gy + d, groups_y)
            copy = result_copy(c, peer, peer, gy, peer)
            copy.wait_send()
            copy.wait_recv()
            return carry

        lax.fori_loop(1, groups_y, finish, 0)


def on_device(volume, conv1_weight, conv1_bias, conv2_weight, conv2_bias):
    groups_x = lax.axis_size("gx")
    groups_y = lax.axis_size("gy")
    cin, planes, in_rows, nz = volume.shape
    cmid = conv1_weight.shape[4]
    cout = conv2_weight.shape[4]
    rows = in_rows // 2
    fw = cout // groups_y
    chunks = 4

    vmem = pl.BlockSpec(memory_space=pltpu.VMEM)
    moved = pl.pallas_call(
        functools.partial(kernel, groups_x, groups_y, chunks),
        out_shape=jax.ShapeDtypeStruct((groups_y, rows, fw, LANES), jnp.bfloat16),
        in_specs=[vmem] * 5,
        out_specs=vmem,
        scratch_shapes=[
            pltpu.VMEM((in_rows + 1, 2, 2, cin, LANES), jnp.bfloat16),
            pltpu.VMEM((rows, cmid, LANES), jnp.bfloat16),
            pltpu.VMEM((rows, cmid, LANES), jnp.bfloat16),
            pltpu.VMEM((rows, cmid, LANES), jnp.float32),
            pltpu.VMEM((rows, cmid, LANES), jnp.bfloat16),
            pltpu.VMEM((rows, cmid, LANES), jnp.bfloat16),
            pltpu.VMEM((rows + 2, 3, cmid, LANES), jnp.bfloat16),
            pltpu.VMEM((rows, groups_y, fw, LANES), jnp.bfloat16),
            pltpu.VMEM((4 * cmid, 12 * cin), jnp.bfloat16),
            pltpu.VMEM((3 * cout, 9 * cmid), jnp.bfloat16),
            pltpu.SemaphoreType.DMA((2,)),
            pltpu.SemaphoreType.DMA((2, chunks)),
            pltpu.SemaphoreType.DMA((2, 2, chunks)),
            pltpu.SemaphoreType.DMA((2, 2, 3)),
            pltpu.SemaphoreType.DMA((chunks, groups_y)),
            pltpu.SemaphoreType.DMA((chunks, groups_y)),
        ],
        compiler_params=pltpu.CompilerParams(
            collective_id=0, has_side_effects=True, vmem_limit_bytes=40 * 1024 * 1024),
    )(volume, conv1_weight, conv1_bias.reshape(cmid, 1), conv2_weight, conv2_bias.reshape(cout, 1))
    return moved.transpose(2, 0, 1, 3).reshape(1, fw, groups_y * rows, LANES)


def solution(mesh):
    return jax.shard_map(
        on_device,
        mesh=mesh,
        in_specs=(P(None, "gx", "gy", None), P(), P(), P(), P()),
        out_specs=P("gx", "gy", None, None),
        check_vma=False,
    )
```

```python
import functools

import jax
import jax.numpy as jnp
from jax import lax
from jax.experimental import pallas as pl
from jax.experimental.pallas import tpu as pltpu
from jax.sharding import PartitionSpec as P

leak_slope = 0.3
MESH = pl.DeviceIdType.MESH
LANES = 128


def leaky(values):
    return jnp.where(values > 0, values, leak_slope * values)


def shift_right(values):
    lane = lax.broadcasted_iota(jnp.int32, values.shape, 1)
    return jnp.where(lane == 0, 0.0, pltpu.roll(values, 1, 1))


def shift_left(values):
    lane = lax.broadcasted_iota(jnp.int32, values.shape, 1)
    return jnp.where(lane == LANES - 1, 0.0, pltpu.roll(values, LANES - 1, 1))


def kernel(groups_x, groups_y, vol_hbm, first_hbm, b1, second_hbm, b2, out,
           vol, first_weight, second_weight,
           cells, part_out, part_in, own, feats, result, w1, w2,
           load_sems, cell_sems, part_sems, feat_sems, edge_sems, send_sems, recv_sems):
    gx = lax.axis_index("gx")
    gy = lax.axis_index("gy")
    has_left = gx > 0
    has_right = gx < groups_x - 1
    has_up = gy > 0
    has_down = gy < groups_y - 1
    rows = own.shape[0]
    step = 2
    chunks = rows // step
    order = [chunks - 1, chunks - 2, 0] + list(range(chunks - 3, 0, -1))
    lag = 2
    in_rows = vol.shape[2]
    cin = vol.shape[0]
    cmid = own.shape[1]
    fw = result.shape[2]

    blocks = in_rows // 16
    loads = [pltpu.make_async_copy(first_hbm, first_weight, load_sems.at[0])]
    for block in reversed(range(blocks)):
        span = pl.ds(block * 16, 16)
        loads.append(pltpu.make_async_copy(
            vol_hbm.at[:, :, span], vol.at[:, :, span], load_sems.at[1 + block]))
    loads.append(pltpu.make_async_copy(second_hbm, second_weight, load_sems.at[1 + blocks]))
    for load in loads:
        load.start()

    feats[...] = jnp.zeros_like(feats)
    part_in[...] = jnp.zeros_like(part_in)
    cells[0] = jnp.zeros(cells.shape[1:], cells.dtype)

    barrier = pltpu.get_barrier_semaphore()

    def greet(x, y):
        pl.semaphore_signal(barrier, inc=1, device_id=(x, y), device_id_type=MESH)

    for d in range(1, groups_y):
        greet(gx, lax.rem(gy + d, groups_y))
    for dx, okx in ((-1, has_left), (1, has_right)):
        for dy, oky in ((-1, has_up), (0, None), (1, has_down)):
            @pl.when(okx if oky is None else jnp.logical_and(okx, oky))
            def _():
                greet(gx + dx, gy + dy)

    sides_y = 1 + has_up.astype(jnp.int32) + has_down.astype(jnp.int32)
    sides_x = has_left.astype(jnp.int32) + has_right.astype(jnp.int32)

    loads[0].wait()

    def turned(pieces):
        return jnp.concatenate(pieces, axis=0).astype(jnp.float32).T.astype(jnp.bfloat16)

    blank = jnp.zeros((cin, cmid), jnp.bfloat16)
    taps = [(b, p, q) for b in range(3) for p in range(2) for q in range(2)]
    kinds = (
        [first_weight[p + 1, b, q + 1] for b, p, q in taps],
        [first_weight[p + 1, b, 0] if q == 1 else blank for b, p, q in taps],
        [first_weight[0, b, q + 1] if p == 1 else blank for b, p, q in taps],
        [first_weight[0, b, 0] if p == 1 and q == 1 else blank for b, p, q in taps],
    )
    for place, pieces in enumerate(kinds):
        w1[place * cmid:(place + 1) * cmid, :] = turned(pieces)

    row = lax.broadcasted_iota(jnp.int32, (2 * LANES, 2 * LANES), 0)
    col = lax.broadcasted_iota(jnp.int32, (2 * LANES, 2 * LANES), 1)
    picked = jnp.where(col < LANES, 2 * col, 2 * col - (2 * LANES - 1))
    select = (row == picked).astype(jnp.float32).astype(jnp.bfloat16)

    def split(block):
        loads[blocks - block].wait()
        for p in range(2):
            part = vol[:, p, pl.ds(block * 16, 16), :].astype(jnp.float32)
            turned = jnp.swapaxes(part, 0, 1).astype(jnp.bfloat16)
            flat = turned.reshape(16 * cin, 2 * LANES)
            both = jnp.dot(flat, select, preferred_element_type=jnp.float32)
            both = both.astype(jnp.bfloat16)
            for q in range(2):
                cells[pl.ds(1 + block * 16, 16), p, q] = (
                    both[:, q * LANES:(q + 1) * LANES].reshape(16, cin, LANES))

    split(blocks - 1)
    pl.semaphore_wait(barrier, groups_y - 1 + sides_x * sides_y)

    def cell_copy(y):
        return pltpu.make_async_remote_copy(
            src_ref=cells.at[in_rows], dst_ref=cells.at[0],
            send_sem=cell_sems.at[0], recv_sem=cell_sems.at[1],
            device_id=(gx, y), device_id_type=MESH)

    @pl.when(has_down)
    def _():
        cell_copy(gy + 1).start()

    def part_copy(c, x):
        span = pl.ds(c * step, step)
        return pltpu.make_async_remote_copy(
            src_ref=part_out.at[span], dst_ref=part_in.at[span],
            send_sem=part_sems.at[0, c], recv_sem=part_sems.at[1, c],
            device_id=(x, gy), device_id_type=MESH)

    def first_rows(j):
        window = jnp.concatenate(
            [cells[2 * (j + h):2 * (j + h) + 3].reshape(12 * cin, LANES) for h in range(2)], axis=1)
        y = jnp.dot(w1[...], window, preferred_element_type=jnp.float32)
        for h in range(2):
            z = y[:, h * LANES:(h + 1) * LANES]
            own[j + h] = z[:cmid] + shift_right(z[cmid:2 * cmid])
            part_out[j + h] = (
                z[2 * cmid:3 * cmid] + shift_right(z[3 * cmid:])).astype(jnp.bfloat16)

    ready = blocks - 1
    for c in order:
        while ready > 0 and 2 * c * step - 1 < ready * 16:
            ready -= 1
            split(ready)
        if c == 0:
            @pl.when(has_up)
            def _():
                cell_copy(gy).wait_recv()
        first_rows(c * step)

        @pl.when(has_right)
        def _():
            part_copy(c, gx + 1).start()

    loads[-1].wait()
    filters = w2.shape[0] // 3
    for e in range(3):
        w2[e * filters:(e + 1) * filters, :] = turned(
            [second_weight[a, b, e] for b in range(3) for a in range(3)])

    def feat_copy(c, side, x):
        span = pl.ds(1 + c * step, step)
        return pltpu.make_async_remote_copy(
            src_ref=feats.at[span, 1], dst_ref=feats.at[span, 2 - 2 * side],
            send_sem=feat_sems.at[0, side, c], recv_sem=feat_sems.at[1, side, c],
            device_id=(x, gy), device_id_type=MESH)

    def edge_copy(down, dx, x, y):
        return pltpu.make_async_remote_copy(
            src_ref=feats.at[rows if down else 1, 1],
            dst_ref=feats.at[0 if down else rows + 1, 1 - dx],
            send_sem=edge_sems.at[0, down, dx + 1], recv_sem=edge_sems.at[1, down, dx + 1],
            device_id=(x, y), device_id_type=MESH)

    def both_of(a, b):
        return b if a is None else jnp.logical_and(a, b)

    def send_edges(down):
        for dx, okx in ((0, None), (-1, has_left), (1, has_right)):
            @pl.when(both_of(okx, has_down if down else has_up))
            def _():
                edge_copy(down, dx, gx + dx, gy + (1 if down else -1)).start()

    def result_copy(c, peer, src_group, y, sem_peer):
        span = pl.ds(c * 2 * step, 2 * step)
        return pltpu.make_async_remote_copy(
            src_ref=result.at[span, peer], dst_ref=out.at[src_group, span],
            send_sem=send_sems.at[c, peer], recv_sem=recv_sems.at[c, sem_peer],
            device_id=(gx, y), device_id_type=MESH)

    def second_rows(j):
        window = jnp.concatenate(
            [feats[j + h:j + h + 3].reshape(9 * cmid, LANES) for h in range(2)], axis=1)
        y = jnp.dot(w2[...], window, preferred_element_type=jnp.float32)
        for h in range(2):
            z = y[:, h * LANES:(h + 1) * LANES]
            total = (shift_right(z[:filters]) + z[filters:2 * filters]
                     + shift_left(z[2 * filters:]) + b2[...])
            result[j + h] = leaky(total).reshape(groups_y, fw, LANES).astype(jnp.bfloat16)

    def finish_chunk(c):
        @pl.when(has_left)
        def _():
            part_copy(c, gx).wait_recv()
        for j in range(c * step, (c + 1) * step):
            value = own[j] + part_in[j].astype(jnp.float32) + b1[...]
            feats[j + 1, 1] = leaky(value).astype(jnp.bfloat16)

        @pl.when(has_left)
        def _():
            feat_copy(c, 0, gx - 1).start()

        @pl.when(has_right)
        def _():
            feat_copy(c, 1, gx + 1).start()
        if c == chunks - 1:
            send_edges(1)
        if c == 0:
            send_edges(0)

    def wait_feats(c):
        @pl.when(has_right)
        def _():
            feat_copy(c, 0, gx).wait_recv()

        @pl.when(has_left)
        def _():
            feat_copy(c, 1, gx).wait_recv()

    def wait_edges(down):
        for dx, okx in ((0, None), (-1, has_right), (1, has_left)):
            @pl.when(both_of(okx, has_up if down else has_down))
            def _():
                edge_copy(down, dx, gx, gy).wait_recv()

    arrived = set()

    def second_chunk(c):
        for near in (c - 1, c, c + 1):
            if 0 <= near < chunks and near not in arrived:
                arrived.add(near)
                wait_feats(near)
        if c == chunks - 1:
            wait_edges(0)
        if c == 0:
            wait_edges(1)
        second_rows(c * step)
        if c % 2 == 0:
            def send(d, carry):
                peer = lax.rem(gy + d, groups_y)
                result_copy(c // 2, peer, gy, peer, gy).start()
                return carry

            lax.fori_loop(1, groups_y, send, 0)

    def ready_at(c):
        needed = [near for near in (c - 1, c, c + 1) if 0 <= near < chunks]
        needed.append(0)
        return max(order.index(near) for near in needed)

    left = list(range(chunks - 1, -1, -1))
    for place, c in enumerate(order):
        finish_chunk(c)
        if left and ready_at(left[0]) + lag <= place:
            second_chunk(left.pop(0))
    for c in left:
        second_chunk(c)

    out[gy] = result[:, gy]

    @pl.when(has_down)
    def _():
        cell_copy(gy).wait_send()

    for c in range(chunks):
        @pl.when(has_right)
        def _():
            part_copy(c, gx).wait_send()
            feat_copy(c, 1, gx).wait_send()

        @pl.when(has_left)
        def _():
            feat_copy(c, 0, gx).wait_send()

    for down in range(2):
        for dx, okx in ((0, None), (-1, has_left), (1, has_right)):
            @pl.when(both_of(okx, has_down if down else has_up))
            def _():
                edge_copy(down, dx, gx, gy).wait_send()

    for c in reversed(range(chunks // 2)):
        def finish(d, carry):
            peer = lax.rem(gy + d, groups_y)
            copy = result_copy(c, peer, peer, gy, peer)
            copy.wait_send()
            copy.wait_recv()
            return carry

        lax.fori_loop(1, groups_y, finish, 0)


def on_device(volume, conv1_weight, conv1_bias, conv2_weight, conv2_bias):
    groups_x = lax.axis_size("gx")
    groups_y = lax.axis_size("gy")
    cin, planes, in_rows, nz = volume.shape
    cmid = conv1_weight.shape[4]
    cout = conv2_weight.shape[4]
    rows = in_rows // 2
    fw = cout // groups_y
    chunks = rows // 2

    vmem = pl.BlockSpec(memory_space=pltpu.VMEM)
    hbm = pl.BlockSpec(memory_space=pltpu.HBM)
    moved = pl.pallas_call(
        functools.partial(kernel, groups_x, groups_y),
        out_shape=jax.ShapeDtypeStruct((groups_y, rows, fw, LANES), jnp.bfloat16),
        in_specs=[hbm, hbm, vmem, hbm, vmem],
        out_specs=vmem,
        scratch_shapes=[
            pltpu.VMEM(volume.shape, jnp.bfloat16),
            pltpu.VMEM(conv1_weight.shape, jnp.bfloat16),
            pltpu.VMEM(conv2_weight.shape, jnp.bfloat16),
            pltpu.VMEM((in_rows + 1, 2, 2, cin, LANES), jnp.bfloat16),
            pltpu.VMEM((rows, cmid, LANES), jnp.bfloat16),
            pltpu.VMEM((rows, cmid, LANES), jnp.bfloat16),
            pltpu.VMEM((rows, cmid, LANES), jnp.float32),
            pltpu.VMEM((rows + 2, 3, cmid, LANES), jnp.bfloat16),
            pltpu.VMEM((rows, groups_y, fw, LANES), jnp.bfloat16),
            pltpu.VMEM((4 * cmid, 12 * cin), jnp.bfloat16),
            pltpu.VMEM((3 * cout, 9 * cmid), jnp.bfloat16),
            pltpu.SemaphoreType.DMA((2 + in_rows // 16,)),
            pltpu.SemaphoreType.DMA((2,)),
            pltpu.SemaphoreType.DMA((2, chunks)),
            pltpu.SemaphoreType.DMA((2, 2, chunks)),
            pltpu.SemaphoreType.DMA((2, 2, 3)),
            pltpu.SemaphoreType.DMA((chunks // 2, groups_y)),
            pltpu.SemaphoreType.DMA((chunks // 2, groups_y)),
        ],
        compiler_params=pltpu.CompilerParams(
            collective_id=0, has_side_effects=True, vmem_limit_bytes=60 * 1024 * 1024),
    )(volume, conv1_weight, conv1_bias.reshape(cmid, 1), conv2_weight, conv2_bias.reshape(cout, 1))
    return moved.transpose(2, 0, 1, 3).reshape(1, fw, groups_y * rows, LANES)


def solution(mesh):
    return jax.shard_map(
        on_device,
        mesh=mesh,
        in_specs=(P(None, "gx", "gy", None), P(), P(), P(), P()),
        out_specs=P("gx", "gy", None, None),
        check_vma=False,
    )
```

```python
import functools

import jax
import jax.numpy as jnp
from jax import lax
from jax.experimental import pallas as pl
from jax.experimental.pallas import tpu as pltpu
from jax.sharding import PartitionSpec as P

leak_slope = 0.3
MESH = pl.DeviceIdType.MESH
LANES = 128


def leaky(values):
    return jnp.where(values > 0, values, leak_slope * values)


def shift_right(values):
    lane = lax.broadcasted_iota(jnp.int32, values.shape, 1)
    return jnp.where(lane == 0, 0.0, pltpu.roll(values, 1, 1))


def shift_left(values):
    lane = lax.broadcasted_iota(jnp.int32, values.shape, 1)
    return jnp.where(lane == LANES - 1, 0.0, pltpu.roll(values, LANES - 1, 1))


def kernel(groups_x, groups_y, vol_hbm, first_hbm, b1_hbm, second_hbm, b2_hbm, out,
           vol, first_weight, second_weight, first_bias, second_bias, b1, b2, relay,
           cells, part_out, part_in, own, feats, result, w1, w2,
           load_sems, cell_sems, part_sems, feat_sems, edge_sems, relay_sems, send_sems, recv_sems):
    gx = lax.axis_index("gx")
    gy = lax.axis_index("gy")
    has_left = gx > 0
    has_right = gx < groups_x - 1
    has_up = gy > 0
    has_down = gy < groups_y - 1
    rows = own.shape[0]
    step = 2
    chunks = rows // step
    order = [chunks - 1, chunks - 2, 0] + list(range(chunks - 3, 0, -1))
    lag = 2
    in_rows = vol.shape[2]
    cin = vol.shape[0]
    cmid = own.shape[1]
    fw = result.shape[2]

    blocks = in_rows // 16
    loads = [pltpu.make_async_copy(first_hbm, first_weight, load_sems.at[0])]
    for block in reversed(range(blocks)):
        span = pl.ds(block * 16, 16)
        loads.append(pltpu.make_async_copy(
            vol_hbm.at[:, :, span], vol.at[:, :, span], load_sems.at[1 + block]))
    loads.append(pltpu.make_async_copy(second_hbm, second_weight, load_sems.at[1 + blocks]))
    loads.append(pltpu.make_async_copy(b1_hbm, first_bias, load_sems.at[2 + blocks]))
    loads.append(pltpu.make_async_copy(b2_hbm, second_bias, load_sems.at[3 + blocks]))
    for load in loads:
        load.start()

    feats[...] = jnp.zeros_like(feats)
    part_in[...] = jnp.zeros_like(part_in)
    cells[0] = jnp.zeros(cells.shape[1:], cells.dtype)

    barrier = pltpu.get_barrier_semaphore()

    def greet(x, y):
        pl.semaphore_signal(barrier, inc=1, device_id=(x, y), device_id_type=MESH)

    for d in range(1, groups_y):
        greet(gx, lax.rem(gy + d, groups_y))
    for dx, okx in ((-1, has_left), (1, has_right)):
        for dy, oky in ((-1, has_up), (0, None), (1, has_down)):
            @pl.when(okx if oky is None else jnp.logical_and(okx, oky))
            def _():
                greet(gx + dx, gy + dy)

    round_about = groups_x == 4
    if round_about:
        greet(lax.rem(gx + 2, 4), gy)

    sides_y = 1 + has_up.astype(jnp.int32) + has_down.astype(jnp.int32)
    sides_x = has_left.astype(jnp.int32) + has_right.astype(jnp.int32)

    loads[0].wait()

    def turned(pieces):
        return jnp.concatenate(pieces, axis=0).astype(jnp.float32).T.astype(jnp.bfloat16)

    blank = jnp.zeros((cin, cmid), jnp.bfloat16)
    taps = [(b, p, q) for b in range(3) for p in range(2) for q in range(2)]
    kinds = (
        [first_weight[p + 1, b, q + 1] for b, p, q in taps],
        [first_weight[p + 1, b, 0] if q == 1 else blank for b, p, q in taps],
        [first_weight[0, b, q + 1] if p == 1 else blank for b, p, q in taps],
        [first_weight[0, b, 0] if p == 1 and q == 1 else blank for b, p, q in taps],
    )
    for place, pieces in enumerate(kinds):
        w1[place * cmid:(place + 1) * cmid, :] = turned(pieces)

    row = lax.broadcasted_iota(jnp.int32, (2 * LANES, 2 * LANES), 0)
    col = lax.broadcasted_iota(jnp.int32, (2 * LANES, 2 * LANES), 1)
    picked = jnp.where(col < LANES, 2 * col, 2 * col - (2 * LANES - 1))
    select = (row == picked).astype(jnp.float32).astype(jnp.bfloat16)

    def split(block):
        loads[blocks - block].wait()
        for p in range(2):
            part = vol[:, p, pl.ds(block * 16, 16), :].astype(jnp.float32)
            turned = jnp.swapaxes(part, 0, 1).astype(jnp.bfloat16)
            flat = turned.reshape(16 * cin, 2 * LANES)
            both = jnp.dot(flat, select, preferred_element_type=jnp.float32)
            both = both.astype(jnp.bfloat16)
            for q in range(2):
                cells[pl.ds(1 + block * 16, 16), p, q] = (
                    both[:, q * LANES:(q + 1) * LANES].reshape(16, cin, LANES))

    split(blocks - 1)
    pl.semaphore_wait(barrier, groups_y - 1 + sides_x * sides_y + (1 if round_about else 0))

    def cell_copy(y):
        return pltpu.make_async_remote_copy(
            src_ref=cells.at[in_rows], dst_ref=cells.at[0],
            send_sem=cell_sems.at[0], recv_sem=cell_sems.at[1],
            device_id=(gx, y), device_id_type=MESH)

    @pl.when(has_down)
    def _():
        cell_copy(gy + 1).start()

    def part_copy(c, x):
        span = pl.ds(c * step, step)
        return pltpu.make_async_remote_copy(
            src_ref=part_out.at[span], dst_ref=part_in.at[span],
            send_sem=part_sems.at[0, c], recv_sem=part_sems.at[1, c],
            device_id=(x, gy), device_id_type=MESH)

    def first_rows(j):
        window = jnp.concatenate(
            [cells[2 * (j + h):2 * (j + h) + 3].reshape(12 * cin, LANES) for h in range(2)], axis=1)
        y = jnp.dot(w1[...], window, preferred_element_type=jnp.float32)
        for h in range(2):
            z = y[:, h * LANES:(h + 1) * LANES]
            own[j + h] = z[:cmid] + shift_right(z[cmid:2 * cmid])
            part_out[j + h] = (
                z[2 * cmid:3 * cmid] + shift_right(z[3 * cmid:])).astype(jnp.bfloat16)

    ready = blocks - 1
    for c in order:
        while ready > 0 and 2 * c * step - 1 < ready * 16:
            ready -= 1
            split(ready)
        if c == 0:
            @pl.when(has_up)
            def _():
                cell_copy(gy).wait_recv()
        first_rows(c * step)

        @pl.when(has_right)
        def _():
            part_copy(c, gx + 1).start()

    for load in loads[-3:]:
        load.wait()
    for bias, spread in ((first_bias, b1), (second_bias, b2)):
        spread[...] = jnp.broadcast_to(bias[...][None, :], (LANES, bias.shape[0])).T

    filters = w2.shape[0] // 3
    for e in range(3):
        w2[e * filters:(e + 1) * filters, :] = turned(
            [second_weight[a, b, e] for b in range(3) for a in range(3)])

    def feat_copy(c, side, x):
        span = pl.ds(1 + c * step, step)
        return pltpu.make_async_remote_copy(
            src_ref=feats.at[span, 1], dst_ref=feats.at[span, 2 - 2 * side],
            send_sem=feat_sems.at[0, side, c], recv_sem=feat_sems.at[1, side, c],
            device_id=(x, gy), device_id_type=MESH)

    def relay_copy(c, x):
        return pltpu.make_async_remote_copy(
            src_ref=feats.at[pl.ds(1 + c * step, step), 1], dst_ref=relay.at[pl.ds(c * step, step)],
            send_sem=relay_sems.at[0, c], recv_sem=relay_sems.at[1, c],
            device_id=(x, gy), device_id_type=MESH)

    def forward_copy(c, side, x):
        return pltpu.make_async_remote_copy(
            src_ref=relay.at[pl.ds(c * step, step)],
            dst_ref=feats.at[pl.ds(1 + c * step, step), 2 - 2 * side],
            send_sem=relay_sems.at[2, c], recv_sem=feat_sems.at[1, side, c],
            device_id=(x, gy), device_id_type=MESH)

    def by_relay(c, side):
        return round_about and (side == 1 or c % 2 == 1)

    def direct(c, side):
        there = has_right if side else has_left
        return jnp.logical_and(there, gx != 2 - side) if by_relay(c, side) else there

    def forward(c):
        for side, middle in ((1, 3), (0, 0)):
            if by_relay(c, side):
                @pl.when(gx == middle)
                def _():
                    relay_copy(c, gx).wait_recv()
                    forward_copy(c, side, 1 + side).start()

    def edge_copy(down, dx, x, y):
        return pltpu.make_async_remote_copy(
            src_ref=feats.at[rows if down else 1, 1],
            dst_ref=feats.at[0 if down else rows + 1, 1 - dx],
            send_sem=edge_sems.at[0, down, dx + 1], recv_sem=edge_sems.at[1, down, dx + 1],
            device_id=(x, y), device_id_type=MESH)

    def both_of(a, b):
        return b if a is None else jnp.logical_and(a, b)

    def send_edges(down):
        for dx, okx in ((0, None), (-1, has_left), (1, has_right)):
            @pl.when(both_of(okx, has_down if down else has_up))
            def _():
                edge_copy(down, dx, gx + dx, gy + (1 if down else -1)).start()

    def result_copy(c, peer, src_group, y, sem_peer):
        span = pl.ds(c * 2 * step, 2 * step)
        return pltpu.make_async_remote_copy(
            src_ref=result.at[span, peer], dst_ref=out.at[src_group, span],
            send_sem=send_sems.at[c, peer], recv_sem=recv_sems.at[c, sem_peer],
            device_id=(gx, y), device_id_type=MESH)

    def second_rows(j):
        window = jnp.concatenate(
            [feats[j + h:j + h + 3].reshape(9 * cmid, LANES) for h in range(2)], axis=1)
        y = jnp.dot(w2[...], window, preferred_element_type=jnp.float32)
        for h in range(2):
            z = y[:, h * LANES:(h + 1) * LANES]
            total = (shift_right(z[:filters]) + z[filters:2 * filters]
                     + shift_left(z[2 * filters:]) + b2[...])
            result[j + h] = leaky(total).reshape(groups_y, fw, LANES).astype(jnp.bfloat16)

    def finish_chunk(c):
        @pl.when(has_left)
        def _():
            part_copy(c, gx).wait_recv()
        for j in range(c * step, (c + 1) * step):
            value = own[j] + part_in[j].astype(jnp.float32) + b1[...]
            feats[j + 1, 1] = leaky(value).astype(jnp.bfloat16)

        for side in range(2):
            @pl.when(direct(c, side))
            def _():
                feat_copy(c, side, gx - 1 + 2 * side).start()

            if by_relay(c, side):
                @pl.when(gx == 2 - side)
                def _():
                    relay_copy(c, 3 * side).start()
        if c == chunks - 1:
            send_edges(1)
        if c == 0:
            send_edges(0)

    def wait_feats(c):
        @pl.when(has_right)
        def _():
            feat_copy(c, 0, gx).wait_recv()

        @pl.when(has_left)
        def _():
            feat_copy(c, 1, gx).wait_recv()

    def wait_edges(down):
        for dx, okx in ((0, None), (-1, has_right), (1, has_left)):
            @pl.when(both_of(okx, has_up if down else has_down))
            def _():
                edge_copy(down, dx, gx, gy).wait_recv()

    arrived = set()

    def second_chunk(c):
        for near in (c - 1, c, c + 1):
            if 0 <= near < chunks and near not in arrived:
                arrived.add(near)
                wait_feats(near)
        if c == chunks - 1:
            wait_edges(0)
        if c == 0:
            wait_edges(1)
        second_rows(c * step)
        if c % 2 == 0:
            def send(d, carry):
                peer = lax.rem(gy + d, groups_y)
                result_copy(c // 2, peer, gy, peer, gy).start()
                return carry

            lax.fori_loop(1, groups_y, send, 0)

    def ready_at(c):
        needed = [near for near in (c - 1, c, c + 1) if 0 <= near < chunks]
        needed.append(0)
        return max(order.index(near) for near in needed)

    left = list(range(chunks - 1, -1, -1))
    for place, c in enumerate(order):
        finish_chunk(c)
        if place > 0:
            forward(order[place - 1])
        if left and ready_at(left[0]) + lag <= place:
            second_chunk(left.pop(0))
    forward(order[-1])
    for c in left:
        second_chunk(c)

    out[gy] = result[:, gy]

    @pl.when(has_down)
    def _():
        cell_copy(gy).wait_send()

    for c in range(chunks):
        @pl.when(has_right)
        def _():
            part_copy(c, gx).wait_send()

        for side in range(2):
            @pl.when(direct(c, side))
            def _():
                feat_copy(c, side, gx).wait_send()

            if by_relay(c, side):
                @pl.when(gx == 2 - side)
                def _():
                    relay_copy(c, gx).wait_send()

                @pl.when(gx == 3 * side)
                def _():
                    forward_copy(c, side, gx).wait_send()

    for down in range(2):
        for dx, okx in ((0, None), (-1, has_left), (1, has_right)):
            @pl.when(both_of(okx, has_down if down else has_up))
            def _():
                edge_copy(down, dx, gx, gy).wait_send()

    for c in reversed(range(chunks // 2)):
        def finish(d, carry):
            peer = lax.rem(gy + d, groups_y)
            copy = result_copy(c, peer, peer, gy, peer)
            copy.wait_send()
            copy.wait_recv()
            return carry

        lax.fori_loop(1, groups_y, finish, 0)


def on_device(volume, conv1_weight, conv1_bias, conv2_weight, conv2_bias):
    groups_x = lax.axis_size("gx")
    groups_y = lax.axis_size("gy")
    cin, planes, in_rows, nz = volume.shape
    cmid = conv1_weight.shape[4]
    cout = conv2_weight.shape[4]
    rows = in_rows // 2
    fw = cout // groups_y
    chunks = rows // 2

    vmem = pl.BlockSpec(memory_space=pltpu.VMEM)
    hbm = pl.BlockSpec(memory_space=pltpu.HBM)
    moved = pl.pallas_call(
        functools.partial(kernel, groups_x, groups_y),
        out_shape=jax.ShapeDtypeStruct((groups_y, rows, fw, LANES), jnp.bfloat16),
        in_specs=[hbm] * 5,
        out_specs=vmem,
        scratch_shapes=[
            pltpu.VMEM(volume.shape, jnp.bfloat16),
            pltpu.VMEM(conv1_weight.shape, jnp.bfloat16),
            pltpu.VMEM(conv2_weight.shape, jnp.bfloat16),
            pltpu.VMEM((cmid,), jnp.float32),
            pltpu.VMEM((cout,), jnp.float32),
            pltpu.VMEM((cmid, LANES), jnp.float32),
            pltpu.VMEM((cout, LANES), jnp.float32),
            pltpu.VMEM((rows, cmid, LANES), jnp.bfloat16),
            pltpu.VMEM((in_rows + 1, 2, 2, cin, LANES), jnp.bfloat16),
            pltpu.VMEM((rows, cmid, LANES), jnp.bfloat16),
            pltpu.VMEM((rows, cmid, LANES), jnp.bfloat16),
            pltpu.VMEM((rows, cmid, LANES), jnp.float32),
            pltpu.VMEM((rows + 2, 3, cmid, LANES), jnp.bfloat16),
            pltpu.VMEM((rows, groups_y, fw, LANES), jnp.bfloat16),
            pltpu.VMEM((4 * cmid, 12 * cin), jnp.bfloat16),
            pltpu.VMEM((3 * cout, 9 * cmid), jnp.bfloat16),
            pltpu.SemaphoreType.DMA((4 + in_rows // 16,)),
            pltpu.SemaphoreType.DMA((2,)),
            pltpu.SemaphoreType.DMA((2, chunks)),
            pltpu.SemaphoreType.DMA((2, 2, chunks)),
            pltpu.SemaphoreType.DMA((2, 2, 3)),
            pltpu.SemaphoreType.DMA((3, chunks)),
            pltpu.SemaphoreType.DMA((chunks // 2, groups_y)),
            pltpu.SemaphoreType.DMA((chunks // 2, groups_y)),
        ],
        compiler_params=pltpu.CompilerParams(
            collective_id=0, has_side_effects=True, vmem_limit_bytes=60 * 1024 * 1024),
    )(volume, conv1_weight, conv1_bias, conv2_weight, conv2_bias)
    return moved.transpose(2, 0, 1, 3).reshape(1, fw, groups_y * rows, LANES)


def solution(mesh):
    return jax.shard_map(
        on_device,
        mesh=mesh,
        in_specs=(P(None, "gx", "gy", None), P(), P(), P(), P()),
        out_specs=P("gx", "gy", None, None),
        check_vma=False,
    )
```

```python
import functools

import jax
import jax.numpy as jnp
from jax import lax
from jax.experimental import pallas as pl
from jax.experimental.pallas import tpu as pltpu
from jax.sharding import PartitionSpec as P

leak_slope = 0.3
MESH = pl.DeviceIdType.MESH
LANES = 128


def leaky(values):
    return jnp.where(values > 0, values, leak_slope * values)


def shift_right(values):
    lane = lax.broadcasted_iota(jnp.int32, values.shape, 1)
    return jnp.where(lane == 0, 0.0, pltpu.roll(values, 1, 1))


def shift_left(values):
    lane = lax.broadcasted_iota(jnp.int32, values.shape, 1)
    return jnp.where(lane == LANES - 1, 0.0, pltpu.roll(values, LANES - 1, 1))


def kernel(groups_x, groups_y, vol_hbm, first_hbm, b1_hbm, second_hbm, b2_hbm, out,
           vol, first_weight, second_weight, first_bias, second_bias, b1, b2, relay,
           cells, part_out, part_in, own, feats, result, w1, w2,
           load_sems, cell_sems, part_sems, feat_sems, edge_sems, relay_sems, send_sems, recv_sems):
    gx = lax.axis_index("gx")
    gy = lax.axis_index("gy")
    has_left = gx > 0
    has_right = gx < groups_x - 1
    has_up = gy > 0
    has_down = gy < groups_y - 1
    rows = own.shape[0]
    step = 2
    chunks = rows // step
    order = [chunks - 1, chunks - 2, 0] + list(range(chunks - 3, 0, -1))
    lag = 2
    in_rows = vol.shape[2]
    cin = vol.shape[0]
    cmid = own.shape[1]
    fw = result.shape[2]

    blocks = in_rows // 16
    loads = [pltpu.make_async_copy(first_hbm, first_weight, load_sems.at[0])]
    for block in reversed(range(blocks)):
        span = pl.ds(block * 16, 16)
        loads.append(pltpu.make_async_copy(
            vol_hbm.at[:, :, span], vol.at[:, :, span], load_sems.at[1 + block]))
    loads.append(pltpu.make_async_copy(second_hbm, second_weight, load_sems.at[1 + blocks]))
    loads.append(pltpu.make_async_copy(b1_hbm, first_bias, load_sems.at[2 + blocks]))
    loads.append(pltpu.make_async_copy(b2_hbm, second_bias, load_sems.at[3 + blocks]))
    for load in loads:
        load.start()

    feats[...] = jnp.zeros_like(feats)
    part_in[...] = jnp.zeros_like(part_in)
    cells[0] = jnp.zeros(cells.shape[1:], cells.dtype)

    barrier = pltpu.get_barrier_semaphore()

    def greet(x, y):
        pl.semaphore_signal(barrier, inc=1, device_id=(x, y), device_id_type=MESH)

    for d in range(1, groups_y):
        greet(gx, lax.rem(gy + d, groups_y))
    for dx, okx in ((-1, has_left), (1, has_right)):
        for dy, oky in ((-1, has_up), (0, None), (1, has_down)):
            @pl.when(okx if oky is None else jnp.logical_and(okx, oky))
            def _():
                greet(gx + dx, gy + dy)

    round_about = groups_x == 4
    if round_about:
        greet(lax.rem(gx + 2, 4), gy)

    sides_y = 1 + has_up.astype(jnp.int32) + has_down.astype(jnp.int32)
    sides_x = has_left.astype(jnp.int32) + has_right.astype(jnp.int32)

    loads[0].wait()

    def turned(pieces):
        return jnp.concatenate(pieces, axis=0).astype(jnp.float32).T.astype(jnp.bfloat16)

    blank = jnp.zeros((cin, cmid), jnp.bfloat16)
    taps = [(b, p, q) for b in range(3) for p in range(2) for q in range(2)]
    kinds = (
        [first_weight[p + 1, b, q + 1] for b, p, q in taps],
        [first_weight[p + 1, b, 0] if q == 1 else blank for b, p, q in taps],
        [first_weight[0, b, q + 1] if p == 1 else blank for b, p, q in taps],
        [first_weight[0, b, 0] if p == 1 and q == 1 else blank for b, p, q in taps],
    )
    for place, pieces in enumerate(kinds):
        w1[place * cmid:(place + 1) * cmid, :] = turned(pieces)

    row = lax.broadcasted_iota(jnp.int32, (2 * LANES, 2 * LANES), 0)
    col = lax.broadcasted_iota(jnp.int32, (2 * LANES, 2 * LANES), 1)
    picked = jnp.where(col < LANES, 2 * col, 2 * col - (2 * LANES - 1))
    select = (row == picked).astype(jnp.float32).astype(jnp.bfloat16)

    def split(block):
        loads[blocks - block].wait()
        for p in range(2):
            part = vol[:, p, pl.ds(block * 16, 16), :].astype(jnp.float32)
            turned = jnp.swapaxes(part, 0, 1).astype(jnp.bfloat16)
            flat = turned.reshape(16 * cin, 2 * LANES)
            both = jnp.dot(flat, select, preferred_element_type=jnp.float32)
            both = both.astype(jnp.bfloat16)
            for q in range(2):
                cells[pl.ds(1 + block * 16, 16), p, q] = (
                    both[:, q * LANES:(q + 1) * LANES].reshape(16, cin, LANES))

    split(blocks - 1)
    pl.semaphore_wait(barrier, groups_y - 1 + sides_x * sides_y + (1 if round_about else 0))

    def cell_copy(y):
        return pltpu.make_async_remote_copy(
            src_ref=cells.at[in_rows], dst_ref=cells.at[0],
            send_sem=cell_sems.at[0], recv_sem=cell_sems.at[1],
            device_id=(gx, y), device_id_type=MESH)

    @pl.when(has_down)
    def _():
        cell_copy(gy + 1).start()

    def part_copy(c, x):
        span = pl.ds(c * step, step)
        return pltpu.make_async_remote_copy(
            src_ref=part_out.at[span], dst_ref=part_in.at[span],
            send_sem=part_sems.at[0, c], recv_sem=part_sems.at[1, c],
            device_id=(x, gy), device_id_type=MESH)

    def first_rows(j):
        window = jnp.concatenate(
            [cells[2 * (j + h):2 * (j + h) + 3].reshape(12 * cin, LANES) for h in range(2)], axis=1)
        y = jnp.dot(w1[...], window, preferred_element_type=jnp.float32)
        for h in range(2):
            z = y[:, h * LANES:(h + 1) * LANES]
            own[j + h] = z[:cmid] + shift_right(z[cmid:2 * cmid])
            part_out[j + h] = (
                z[2 * cmid:3 * cmid] + shift_right(z[3 * cmid:])).astype(jnp.bfloat16)

    split_blocks = {blocks - 1}

    def first_chunk(c):
        for block in reversed(range(blocks)):
            if block not in split_blocks and 2 * c * step - 1 < (block + 1) * 16:
                split_blocks.add(block)
                split(block)
        if c == 0:
            @pl.when(has_up)
            def _():
                cell_copy(gy).wait_recv()
        first_rows(c * step)

        @pl.when(has_right)
        def _():
            part_copy(c, gx + 1).start()

    filters = w2.shape[0] // 3

    def turn_biases():
        for load in loads[-2:]:
            load.wait()
        for bias, spread in ((first_bias, b1), (second_bias, b2)):
            spread[...] = jnp.broadcast_to(bias[...][None, :], (LANES, bias.shape[0])).T

    def turn_second_weight():
        loads[-3].wait()
        for e in range(3):
            w2[e * filters:(e + 1) * filters, :] = turned(
                [second_weight[a, b, e] for b in range(3) for a in range(3)])

    def feat_copy(c, side, x):
        span = pl.ds(1 + c * step, step)
        return pltpu.make_async_remote_copy(
            src_ref=feats.at[span, 1], dst_ref=feats.at[span, 2 - 2 * side],
            send_sem=feat_sems.at[0, side, c], recv_sem=feat_sems.at[1, side, c],
            device_id=(x, gy), device_id_type=MESH)

    def relay_copy(c, x):
        return pltpu.make_async_remote_copy(
            src_ref=feats.at[pl.ds(1 + c * step, step), 1], dst_ref=relay.at[pl.ds(c * step, step)],
            send_sem=relay_sems.at[0, c], recv_sem=relay_sems.at[1, c],
            device_id=(x, gy), device_id_type=MESH)

    def forward_copy(c, side, x):
        return pltpu.make_async_remote_copy(
            src_ref=relay.at[pl.ds(c * step, step)],
            dst_ref=feats.at[pl.ds(1 + c * step, step), 2 - 2 * side],
            send_sem=relay_sems.at[2, c], recv_sem=feat_sems.at[1, side, c],
            device_id=(x, gy), device_id_type=MESH)

    def by_relay(c, side):
        return round_about and (side == 1 or c % 2 == 1)

    def direct(c, side):
        there = has_right if side else has_left
        return jnp.logical_and(there, gx != 2 - side) if by_relay(c, side) else there

    def forward(c):
        for side, middle in ((1, 3), (0, 0)):
            if by_relay(c, side):
                @pl.when(gx == middle)
                def _():
                    relay_copy(c, gx).wait_recv()
                    forward_copy(c, side, 1 + side).start()

    def edge_copy(down, dx, x, y):
        return pltpu.make_async_remote_copy(
            src_ref=feats.at[rows if down else 1, 1],
            dst_ref=feats.at[0 if down else rows + 1, 1 - dx],
            send_sem=edge_sems.at[0, down, dx + 1], recv_sem=edge_sems.at[1, down, dx + 1],
            device_id=(x, y), device_id_type=MESH)

    def both_of(a, b):
        return b if a is None else jnp.logical_and(a, b)

    def send_edges(down):
        for dx, okx in ((0, None), (-1, has_left), (1, has_right)):
            @pl.when(both_of(okx, has_down if down else has_up))
            def _():
                edge_copy(down, dx, gx + dx, gy + (1 if down else -1)).start()

    def result_copy(c, peer, src_group, y, sem_peer):
        span = pl.ds(c * 2 * step, 2 * step)
        return pltpu.make_async_remote_copy(
            src_ref=result.at[span, peer], dst_ref=out.at[src_group, span],
            send_sem=send_sems.at[c, peer], recv_sem=recv_sems.at[c, sem_peer],
            device_id=(gx, y), device_id_type=MESH)

    def second_rows(j):
        window = jnp.concatenate(
            [feats[j + h:j + h + 3].reshape(9 * cmid, LANES) for h in range(2)], axis=1)
        y = jnp.dot(w2[...], window, preferred_element_type=jnp.float32)
        for h in range(2):
            z = y[:, h * LANES:(h + 1) * LANES]
            total = (shift_right(z[:filters]) + z[filters:2 * filters]
                     + shift_left(z[2 * filters:]) + b2[...])
            result[j + h] = leaky(total).reshape(groups_y, fw, LANES).astype(jnp.bfloat16)

    def finish_chunk(c):
        @pl.when(has_left)
        def _():
            part_copy(c, gx).wait_recv()
        for j in range(c * step, (c + 1) * step):
            value = own[j] + part_in[j].astype(jnp.float32) + b1[...]
            feats[j + 1, 1] = leaky(value).astype(jnp.bfloat16)

        for side in range(2):
            @pl.when(direct(c, side))
            def _():
                feat_copy(c, side, gx - 1 + 2 * side).start()

            if by_relay(c, side):
                @pl.when(gx == 2 - side)
                def _():
                    relay_copy(c, 3 * side).start()
        if c == chunks - 1:
            send_edges(1)
        if c == 0:
            send_edges(0)

    def wait_feats(c):
        @pl.when(has_right)
        def _():
            feat_copy(c, 0, gx).wait_recv()

        @pl.when(has_left)
        def _():
            feat_copy(c, 1, gx).wait_recv()

    def wait_edges(down):
        for dx, okx in ((0, None), (-1, has_right), (1, has_left)):
            @pl.when(both_of(okx, has_up if down else has_down))
            def _():
                edge_copy(down, dx, gx, gy).wait_recv()

    arrived = set()

    def second_chunk(c):
        for near in (c - 1, c, c + 1):
            if 0 <= near < chunks and near not in arrived:
                arrived.add(near)
                wait_feats(near)
        if c == chunks - 1:
            wait_edges(0)
        if c == 0:
            wait_edges(1)
        second_rows(c * step)
        if c % 2 == 0:
            def send(d, carry):
                peer = lax.rem(gy + d, groups_y)
                result_copy(c // 2, peer, gy, peer, gy).start()
                return carry

            lax.fori_loop(1, groups_y, send, 0)

    def ready_at(c):
        needed = [near for near in (c - 1, c, c + 1) if 0 <= near < chunks]
        needed.append(0)
        return max(order.index(near) for near in needed)

    left = list(range(chunks - 1, -1, -1))
    behind = min(3, chunks - 1)
    turn_biases()
    for place in range(chunks + behind):
        if place < chunks:
            first_chunk(order[place])
        done = place - behind
        if done < 0:
            continue
        finish_chunk(order[done])
        if done > 0:
            forward(order[done - 1])
        if left and ready_at(left[0]) + lag <= done:
            if len(left) == chunks:
                turn_second_weight()
            second_chunk(left.pop(0))
    forward(order[-1])
    if len(left) == chunks:
        turn_second_weight()
    for c in left:
        second_chunk(c)

    out[gy] = result[:, gy]

    @pl.when(has_down)
    def _():
        cell_copy(gy).wait_send()

    for c in range(chunks):
        @pl.when(has_right)
        def _():
            part_copy(c, gx).wait_send()

        for side in range(2):
            @pl.when(direct(c, side))
            def _():
                feat_copy(c, side, gx).wait_send()

            if by_relay(c, side):
                @pl.when(gx == 2 - side)
                def _():
                    relay_copy(c, gx).wait_send()

                @pl.when(gx == 3 * side)
                def _():
                    forward_copy(c, side, gx).wait_send()

    for down in range(2):
        for dx, okx in ((0, None), (-1, has_left), (1, has_right)):
            @pl.when(both_of(okx, has_down if down else has_up))
            def _():
                edge_copy(down, dx, gx, gy).wait_send()

    for c in reversed(range(chunks // 2)):
        def finish(d, carry):
            peer = lax.rem(gy + d, groups_y)
            copy = result_copy(c, peer, peer, gy, peer)
            copy.wait_send()
            copy.wait_recv()
            return carry

        lax.fori_loop(1, groups_y, finish, 0)


def on_device(volume, conv1_weight, conv1_bias, conv2_weight, conv2_bias):
    groups_x = lax.axis_size("gx")
    groups_y = lax.axis_size("gy")
    cin, planes, in_rows, nz = volume.shape
    cmid = conv1_weight.shape[4]
    cout = conv2_weight.shape[4]
    rows = in_rows // 2
    fw = cout // groups_y
    chunks = rows // 2

    vmem = pl.BlockSpec(memory_space=pltpu.VMEM)
    hbm = pl.BlockSpec(memory_space=pltpu.HBM)
    moved = pl.pallas_call(
        functools.partial(kernel, groups_x, groups_y),
        out_shape=jax.ShapeDtypeStruct((groups_y, rows, fw, LANES), jnp.bfloat16),
        in_specs=[hbm] * 5,
        out_specs=vmem,
        scratch_shapes=[
            pltpu.VMEM(volume.shape, jnp.bfloat16),
            pltpu.VMEM(conv1_weight.shape, jnp.bfloat16),
            pltpu.VMEM(conv2_weight.shape, jnp.bfloat16),
            pltpu.VMEM((cmid,), jnp.float32),
            pltpu.VMEM((cout,), jnp.float32),
            pltpu.VMEM((cmid, LANES), jnp.float32),
            pltpu.VMEM((cout, LANES), jnp.float32),
            pltpu.VMEM((rows, cmid, LANES), jnp.bfloat16),
            pltpu.VMEM((in_rows + 1, 2, 2, cin, LANES), jnp.bfloat16),
            pltpu.VMEM((rows, cmid, LANES), jnp.bfloat16),
            pltpu.VMEM((rows, cmid, LANES), jnp.bfloat16),
            pltpu.VMEM((rows, cmid, LANES), jnp.float32),
            pltpu.VMEM((rows + 2, 3, cmid, LANES), jnp.bfloat16),
            pltpu.VMEM((rows, groups_y, fw, LANES), jnp.bfloat16),
            pltpu.VMEM((4 * cmid, 12 * cin), jnp.bfloat16),
            pltpu.VMEM((3 * cout, 9 * cmid), jnp.bfloat16),
            pltpu.SemaphoreType.DMA((4 + in_rows // 16,)),
            pltpu.SemaphoreType.DMA((2,)),
            pltpu.SemaphoreType.DMA((2, chunks)),
            pltpu.SemaphoreType.DMA((2, 2, chunks)),
            pltpu.SemaphoreType.DMA((2, 2, 3)),
            pltpu.SemaphoreType.DMA((3, chunks)),
            pltpu.SemaphoreType.DMA((chunks // 2, groups_y)),
            pltpu.SemaphoreType.DMA((chunks // 2, groups_y)),
        ],
        compiler_params=pltpu.CompilerParams(
            collective_id=0, has_side_effects=True, vmem_limit_bytes=60 * 1024 * 1024),
    )(volume, conv1_weight, conv1_bias, conv2_weight, conv2_bias)
    return moved.transpose(2, 0, 1, 3).reshape(1, fw, groups_y * rows, LANES)


def solution(mesh):
    return jax.shard_map(
        on_device,
        mesh=mesh,
        in_specs=(P(None, "gx", "gy", None), P(), P(), P(), P()),
        out_specs=P("gx", "gy", None, None),
        check_vma=False,
    )
```
